512 devices in a mesh: dp: 32 (over x, y, core), tensor: 16 (over z).
Axes of the slice: x: 4, y: 4, z: 16, core: 2. Of those that a mesh axis runs over, the one named last changes fastest.
Arguments:
- tokens: bfloat16 [65536, 8192], P('dp', 'tensor'), may hold values from -6 to 6
- grad_out: bfloat16 [65536, 1024], P('dp', 'tensor'), may hold values from -0.14941406 to 0.14941406
- error_old: bfloat16 [32, 1024, 8192], P('dp', None, 'tensor'), may hold values from -3 to 3
- power_q: float32 [8192, 32], P('tensor'), may hold values from -6 to 6
Outputs:
- factor_q: float32 [8192, 32], P('tensor')
- error_new: bfloat16 [32, 1024, 8192], P('dp', None, 'tensor')
The draws below stay inside these ranges and needn't reach their ends.
All inputs are finite; a program needn't handle non-finite values.
Results may differ from the reference program's by a relative error of at most 0.00045.
Values may be sent and summed in bfloat16 or wider, within the bound.
A program may use at most 64 MiB of HBM per device.

```python
import jax
import jax.numpy as jnp
from jax import lax

D = 8192
HD = 1024
RANK = 32
TOK = 2048
TOKENS = 65536
N_DP = 32


def block_scale(rng, dims, pieces, smallest, top_value):
    level = 1.0
    for axis_at, parts in pieces:
        heights = jax.random.uniform(jax.random.fold_in(jax.random.fold_in(rng, 6), axis_at), (parts,), jnp.float32, smallest / len(pieces), top_value / len(pieces))
        level = level * jnp.repeat(jnp.exp(heights), dims[axis_at] // parts).reshape((-1,) + (1,) * (len(dims) - 1 - axis_at))
    return level


def gaussian(own_key, shape, width, reach, cuts=(), kind=jnp.bfloat16):
    array = jax.random.normal(own_key, shape, jnp.float32) * width
    if len(cuts) > 0:
        array = block_scale(own_key, shape, cuts, -0.22, 0.18) * array
    return jnp.clip(array, min=-reach, max=reach).astype(kind)


def setup_inputs(seed: int = 0) -> dict:
    key_of = jax.random.split(jax.random.key(seed), 5)
    tokens = gaussian(key_of[0], (TOKENS, D), 1.0, 6.0, ((0, 32), (1, 16)))
    grad_out = gaussian(key_of[1], (TOKENS, HD), 0.025, 0.14941406, ((0, 32), (1, 16)))
    error_old = gaussian(key_of[2], (N_DP, HD, D), 0.5, 3.0, ((0, 32), (2, 16)))
    power_q = gaussian(key_of[3], (D, RANK), 1.0, 6.0, ((0, 16),), jnp.float32)
    return dict(tokens=tokens, grad_out=grad_out, error_old=error_old, power_q=power_q)


def orthonormal(p_sum):
    gram_matrix = jnp.dot(p_sum.T, p_sum, precision=lax.Precision.HIGHEST)
    cholesky_factor = jnp.linalg.cholesky(gram_matrix)
    return lax.linalg.triangular_solve(cholesky_factor, p_sum, left_side=False, lower=True, transpose_a=True)

def reference(tokens, grad_out, error_old, power_q):

    def replica_grad(index):
        start = (index * TOK).astype(jnp.int32)
        inputs = lax.dynamic_slice_in_dim(tokens, start, TOK, 0)
        cotangent = lax.dynamic_slice_in_dim(grad_out, start, TOK, 0)
        gradient = lax.dot_general(cotangent.astype(jnp.float32), inputs.astype(jnp.float32), (((0,), (0,)), ((), ())), preferred_element_type=jnp.float32)
        return gradient + error_old[index].astype(jnp.float32)
    merged = lax.map(replica_grad, jnp.arange(N_DP, dtype=jnp.int32))
    p_sum = jnp.einsum('rhd,dk->hk', merged, power_q.astype(jnp.float32), precision=lax.Precision.HIGHEST)
    ortho_basis = orthonormal(p_sum)
    factor_q = jnp.einsum('rhd,hk->dk', merged, ortho_basis, precision=lax.Precision.HIGHEST)
    low_rank = jnp.dot(ortho_basis, factor_q.T, precision=lax.Precision.HIGHEST) / N_DP
    error_new = (merged - low_rank[None]).astype(jnp.bfloat16)
    return (factor_q, error_new)
```

```python
import functools

import jax
import jax.numpy as jnp
from jax import lax
from jax.experimental import pallas as pl
from jax.experimental.pallas import tpu as pltpu
from jax.sharding import PartitionSpec as P

F32 = jnp.float32
BF16 = jnp.bfloat16
MESH = pl.DeviceIdType.MESH
HIGHEST = lax.Precision.HIGHEST
NT = (((1,), (1,)), ((), ()))
NN = (((1,), (0,)), ((), ()))
TN = (((0,), (0,)), ((), ()))
PIECES = 4


def split2(x):
    hi = x.astype(BF16)
    return hi, (x - hi.astype(F32)).astype(BF16)


def dot3(a, b, dims):
    a1, a2 = split2(a)
    b1, b2 = split2(b)
    dot = functools.partial(lax.dot_general, dimension_numbers=dims, preferred_element_type=F32)
    return dot(a1, b1) + (dot(a1, b2) + dot(a2, b1))


def kernel(
    nd, nz, gt_hbm, tok_hbm, err_hbm, qt_hbm, fq_hbm, new_hbm,
    gt, tok, err, qt, merged, out, fq,
    part_p, plane_p, deep_p, full_p, part_u, plane_u, full_u,
    load_sem, ring_send, ring_recv, send_sem, recv_sem, store_sem,
):
    dp = lax.axis_index("dp")
    z = lax.axis_index("tensor")
    hb = gt.shape[1]
    rows = hb // PIECES
    half = nz // 2
    rank = qt.shape[0]
    width = qt.shape[1]

    loads = [
        pltpu.make_async_copy(gt_hbm, gt.at[z], load_sem.at[0]),
        pltpu.make_async_copy(tok_hbm, tok, load_sem.at[1]),
        pltpu.make_async_copy(err_hbm, err, load_sem.at[2]),
        pltpu.make_async_copy(qt_hbm, qt, load_sem.at[3]),
    ]
    for load in loads:
        load.start()

    barrier = pltpu.get_barrier_semaphore()

    def greet(axis, n, me):
        def body(k, carry):
            pl.semaphore_signal(
                barrier, inc=1, device_id={axis: lax.rem(me + k, n)}, device_id_type=MESH
            )
            return carry

        lax.fori_loop(1, n, body, 0)

    greet("tensor", nz, z)
    greet("dp", nd, dp)
    pl.semaphore_wait(barrier, nd + nz - 2)

    def ring(way, step, piece):
        sign = 1 if way == 0 else -1
        block = lax.rem(z - sign * step + 2 * nz, nz)
        there = lax.rem(z + sign + nz, nz)
        ref = gt.at[block, pl.ds(piece * rows, rows)]
        return pltpu.make_async_remote_copy(
            src_ref=ref,
            dst_ref=ref,
            send_sem=ring_send.at[way, step, piece],
            recv_sem=ring_recv.at[way, step, piece],
            device_id={"tensor": there},
            device_id_type=MESH,
        )

    def arrived(way, step, piece):
        sign = 1 if way == 0 else -1
        block = lax.rem(z - sign * (step + 1) + 2 * nz, nz)
        ref = gt.at[block, pl.ds(piece * rows, rows)]
        pltpu.make_async_copy(ref, ref, ring_recv.at[way, step, piece]).wait()

    def multiply(block_a, block_b=None):
        x = gt[block_a]
        if block_b is not None:
            x = jnp.concatenate([x, gt[block_b]], axis=0)
        y = jnp.dot(x, tok[...], preferred_element_type=F32)
        merged[block_a] = y[:hb] + err[block_a].astype(F32)
        if block_b is not None:
            merged[block_b] = y[hb:] + err[block_b].astype(F32)

    loads[0].wait()
    for piece in range(PIECES):
        ring(0, 0, piece).start()
        ring(1, 0, piece).start()
    for load in loads[1:]:
        load.wait()
    multiply(z)

    def step_body(s, carry):
        for piece in range(PIECES):
            for way in range(2):
                arrived(way, s - 1, piece)
                ring(way, s, piece).start()
        multiply(lax.rem(z + s, nz), lax.rem(z - s + nz, nz))
        return carry

    lax.fori_loop(1, half - 1, step_body, 0)
    s = half - 1
    for piece in range(PIECES):
        for way in range(2):
            arrived(way, s - 1, piece)
            if (piece < PIECES // 2) == (way == 0):
                ring(way, s, piece).start()
    multiply(lax.rem(z + s, nz), lax.rem(z - s + nz, nz))
    for piece in range(PIECES):
        arrived(0 if piece < PIECES // 2 else 1, s, piece)
    multiply(lax.rem(z + half, nz))

    hd = nz * hb
    part = dot3(qt[...], merged[...].reshape(hd, width), NT)

    def exchange(axis, n, me, sems, source, target):
        def one(k):
            there = lax.rem(me + k, n)
            return pltpu.make_async_remote_copy(
                src_ref=source(there),
                dst_ref=target.at[me],
                send_sem=send_sem.at[sems],
                recv_sem=recv_sem.at[sems],
                device_id={axis: there},
                device_id_type=MESH,
            )

        def body(k, carry):
            one(k).start()
            return carry

        lax.fori_loop(1, n, body, 0)

    def landed(sems, n, target):
        rest = target.at[pl.ds(0, n - 1)]
        pltpu.make_async_copy(rest, rest, recv_sem.at[sems]).wait()

    def left(sems, n, target):
        rest = target.at[pl.ds(0, n - 1)]
        pltpu.make_async_copy(rest, rest, send_sem.at[sems]).wait()

    tiles = hd // 128
    for i in range(rank // 8):
        for j in range(tiles):
            part_p[i * tiles + j] = part[i * 8 : i * 8 + 8, j * 128 : j * 128 + 128]
    plane_p[dp] = part_p[dp]
    exchange("dp", nd, dp, 0, lambda there: part_p.at[there], plane_p)
    landed(0, nd, plane_p)
    deep_p[z] = jnp.sum(plane_p[...], axis=0)
    exchange("tensor", nz, z, 1, lambda there: deep_p.at[z], deep_p)
    landed(1, nz, deep_p)
    full_p[dp] = jnp.sum(deep_p[...], axis=0)
    exchange("dp", nd, dp, 2, lambda there: full_p.at[dp], full_p)
    landed(2, nd, full_p)
    pt = jnp.concatenate(
        [
            jnp.concatenate([full_p[i * tiles + j] for j in range(tiles)], axis=1)
            for i in range(rank // 8)
        ],
        axis=0,
    )

    ut = dot3(pt, merged[...].reshape(hd, width), NN)
    urows = part_u.shape[1]
    utiles = width // 128
    for i in range(rank // urows):
        for j in range(utiles):
            part_u[i * utiles + j] = ut[i * urows : (i + 1) * urows, j * 128 : j * 128 + 128]
    plane_u[dp] = part_u[dp]
    exchange("dp", nd, dp, 3, lambda there: part_u.at[there], plane_u)

    gram = lax.dot_general(pt, pt, NT, precision=HIGHEST, preferred_element_type=F32)
    row_id = lax.broadcasted_iota(jnp.int32, (rank, 1), 0)
    eye = (
        lax.broadcasted_iota(jnp.int32, (rank, rank), 0)
        == lax.broadcasted_iota(jnp.int32, (rank, rank), 1)
    ).astype(F32)
    x = jnp.concatenate([gram, eye], axis=1)

    def eliminate(x, start, stop):
        for k in range(start, stop):
            d = x[k : k + 1, k : k + 1]
            r = lax.rsqrt(d)
            r = r * (1.5 - 0.5 * d * r * r)
            row = x[k : k + 1, :] * r
            column = x[:, k : k + 1] * r
            x = jnp.where(row_id == k, row, jnp.where(row_id > k, x - column * row, x))
        return x

    x = eliminate(x, 0, rank // 2)
    landed(3, nd, plane_u)
    full_u[dp] = jnp.sum(plane_u[...], axis=0)
    exchange("dp", nd, dp, 4, lambda there: full_u.at[dp], full_u)
    x = eliminate(x, rank // 2, rank)
    inverse = x[:, rank:]
    landed(4, nd, full_u)
    ut = jnp.concatenate(
        [
            jnp.concatenate([full_u[i * utiles + j] for j in range(utiles)], axis=1)
            for i in range(rank // urows)
        ],
        axis=0,
    )
    fqt = lax.dot_general(inverse, ut, NN, precision=HIGHEST, preferred_element_type=F32)
    fq[...] = fqt
    fq_store = pltpu.make_async_copy(fq, fq_hbm, store_sem.at[0])
    fq_store.start()
    mix = lax.dot_general(inverse, fqt, TN, precision=HIGHEST, preferred_element_type=F32) / nd
    p1, p2 = split2(pt)
    m1, m2 = split2(mix)
    left_side = jnp.concatenate([p1, p1, p2], axis=0)
    right_side = jnp.concatenate([m1, m2, m1], axis=0)
    stores = []
    groups = 4
    per = nz // groups
    for g in range(groups):
        n = per * hb
        low = lax.dot_general(
            left_side[:, g * n : (g + 1) * n], right_side, TN, preferred_element_type=F32
        )
        at = pl.ds(g * per, per)
        out[at] = (merged[at] - low.reshape(per, hb, width)).astype(BF16)
        store = pltpu.make_async_copy(out.at[at], new_hbm.at[at], store_sem.at[1 + g])
        store.start()
        stores.append(store)

    def sent(s, carry):
        for piece in range(PIECES):
            for way in range(2):
                ring(way, s, piece).wait_send()
        return carry

    lax.fori_loop(0, half - 1, sent, 0)
    for piece in range(PIECES):
        ring(0 if piece < PIECES // 2 else 1, half - 1, piece).wait_send()
    left(0, nd, plane_p)
    left(1, nz, deep_p)
    left(2, nd, full_p)
    left(3, nd, plane_u)
    left(4, nd, full_u)
    fq_store.wait()
    for store in stores:
        store.wait()


def local(nd, nz, tokens, grad_out, error_old, power_q):
    tok_n, hb = grad_out.shape
    width = tokens.shape[1]
    rank = power_q.shape[1]
    hd = hb * nz
    chunk = rank * hd // nd // 128
    urows = rank * width // nd // 128
    any_space = pl.BlockSpec(memory_space=pl.ANY)
    fqt, new = pl.pallas_call(
        functools.partial(kernel, nd, nz),
        out_shape=(
            jax.ShapeDtypeStruct((rank, width), F32),
            jax.ShapeDtypeStruct((nz, hb, width), BF16),
        ),
        in_specs=[any_space] * 4,
        out_specs=(any_space, any_space),
        scratch_shapes=[
            pltpu.VMEM((nz, hb, tok_n), BF16),
            pltpu.VMEM((tok_n, width), BF16),
            pltpu.VMEM((nz, hb, width), BF16),
            pltpu.VMEM((rank, width), F32),
            pltpu.VMEM((nz, hb, width), F32),
            pltpu.VMEM((nz, hb, width), BF16),
            pltpu.VMEM((rank, width), F32),
            pltpu.VMEM((nd, chunk, 128), F32),
            pltpu.VMEM((nd, chunk, 128), F32),
            pltpu.VMEM((nz, chunk, 128), F32),
            pltpu.VMEM((nd, chunk, 128), F32),
            pltpu.VMEM((nd, urows, 128), F32),
            pltpu.VMEM((nd, urows, 128), F32),
            pltpu.VMEM((nd, urows, 128), F32),
            pltpu.SemaphoreType.DMA((4,)),
            pltpu.SemaphoreType.DMA((2, nz // 2, PIECES)),
            pltpu.SemaphoreType.DMA((2, nz // 2, PIECES)),
            pltpu.SemaphoreType.DMA((5,)),
            pltpu.SemaphoreType.DMA((5,)),
            pltpu.SemaphoreType.DMA((5,)),
        ],
        compiler_params=pltpu.CompilerParams(
            collective_id=0, has_side_effects=True, vmem_limit_bytes=48 * 1024 * 1024
        ),
    )(grad_out.T, tokens, error_old.reshape(nz, hb, width), power_q.T)
    return fqt.T, new.reshape(1, hd, width)


def solution(mesh):
    placed = (P("dp", "tensor"), P("dp", "tensor"), P("dp", None, "tensor"), P("tensor", None))
    return jax.shard_map(
        functools.partial(local, mesh.shape["dp"], mesh.shape["tensor"]),
        mesh=mesh,
        in_specs=placed,
        out_specs=(P("tensor", None), P("dp", None, "tensor")),
        check_vma=False,
    )
```

```python
import functools

import jax
import jax.numpy as jnp
from jax import lax
from jax.experimental import pallas as pl
from jax.experimental.pallas import tpu as pltpu
from jax.sharding import PartitionSpec as P

F32 = jnp.float32
BF16 = jnp.bfloat16
MESH = pl.DeviceIdType.MESH
HIGHEST = lax.Precision.HIGHEST
NT = (((1,), (1,)), ((), ()))
NN = (((1,), (0,)), ((), ()))
TN = (((0,), (0,)), ((), ()))
PIECES = 4


def split2(x):
    hi = x.astype(BF16)
    return hi, (x - hi.astype(F32)).astype(BF16)


def dot3(a, b, dims):
    a1, a2 = split2(a)
    b1, b2 = split2(b)
    dot = functools.partial(lax.dot_general, dimension_numbers=dims, preferred_element_type=F32)
    return dot(a1, b1) + (dot(a1, b2) + dot(a2, b1))


def kernel(
    nd, nz, gt_hbm, tok_hbm, err_hbm, qt_hbm, fq_hbm, new_hbm,
    gt, tok, err, qt, merged, out, fq,
    part_p, plane_p, deep_p, full_p, part_u, plane_u, full_u,
    load_sem, ring_send, ring_recv, send_sem, recv_sem, store_sem,
):
    dp = lax.axis_index("dp")
    z = lax.axis_index("tensor")
    hb = gt.shape[1]
    rows = hb // PIECES
    half = nz // 2
    rank = qt.shape[0]
    width = qt.shape[1]

    loads = [
        pltpu.make_async_copy(gt_hbm, gt.at[z], load_sem.at[0]),
        pltpu.make_async_copy(tok_hbm, tok, load_sem.at[1]),
        pltpu.make_async_copy(err_hbm, err, load_sem.at[2]),
        pltpu.make_async_copy(qt_hbm, qt, load_sem.at[3]),
    ]
    for load in loads:
        load.start()

    barrier = pltpu.get_barrier_semaphore()

    def greet(axis, n, me):
        def body(k, carry):
            pl.semaphore_signal(
                barrier, inc=1, device_id={axis: lax.rem(me + k, n)}, device_id_type=MESH
            )
            return carry

        lax.fori_loop(1, n, body, 0)

    for step in (1, nz - 1):
        pl.semaphore_signal(
            barrier, inc=1, device_id={"tensor": lax.rem(z + step, nz)}, device_id_type=MESH
        )
    greet("dp", nd, dp)
    pl.semaphore_wait(barrier, nd + 1)

    def ring(way, step, piece):
        sign = 1 if way == 0 else -1
        block = lax.rem(z - sign * step + 2 * nz, nz)
        there = lax.rem(z + sign + nz, nz)
        ref = gt.at[block, pl.ds(piece * rows, rows)]
        return pltpu.make_async_remote_copy(
            src_ref=ref,
            dst_ref=ref,
            send_sem=ring_send.at[way, step, piece],
            recv_sem=ring_recv.at[way, step, piece],
            device_id={"tensor": there},
            device_id_type=MESH,
        )

    def arrived(way, step, piece):
        sign = 1 if way == 0 else -1
        block = lax.rem(z - sign * (step + 1) + 2 * nz, nz)
        ref = gt.at[block, pl.ds(piece * rows, rows)]
        pltpu.make_async_copy(ref, ref, ring_recv.at[way, step, piece]).wait()

    def multiply(block_a, block_b=None):
        x = gt[block_a]
        if block_b is not None:
            x = jnp.concatenate([x, gt[block_b]], axis=0)
        y = jnp.dot(x, tok[...], preferred_element_type=F32)
        merged[block_a] = y[:hb] + err[block_a].astype(F32)
        if block_b is not None:
            merged[block_b] = y[hb:] + err[block_b].astype(F32)

    loads[0].wait()
    for piece in range(PIECES):
        ring(0, 0, piece).start()
        ring(1, 0, piece).start()
    for load in loads[1:]:
        load.wait()
    multiply(z)

    def step_body(s, carry):
        for piece in range(PIECES):
            for way in range(2):
                arrived(way, s - 1, piece)
                ring(way, s, piece).start()
        multiply(lax.rem(z + s, nz), lax.rem(z - s + nz, nz))
        return carry

    lax.fori_loop(1, half - 1, step_body, 0)
    s = half - 1
    for piece in range(PIECES):
        for way in range(2):
            arrived(way, s - 1, piece)
            if (piece < PIECES // 2) == (way == 0):
                ring(way, s, piece).start()
    multiply(lax.rem(z + s, nz), lax.rem(z - s + nz, nz))
    for piece in range(PIECES):
        arrived(0 if piece < PIECES // 2 else 1, s, piece)
    multiply(lax.rem(z + half, nz))

    hd = nz * hb
    part = dot3(qt[...], merged[...].reshape(hd, width), NT)

    def exchange(axis, n, me, sems, source, target):
        def one(k):
            there = lax.rem(me + k, n)
            return pltpu.make_async_remote_copy(
                src_ref=source(there),
                dst_ref=target.at[me],
                send_sem=send_sem.at[sems],
                recv_sem=recv_sem.at[sems],
                device_id={axis: there},
                device_id_type=MESH,
            )

        def body(k, carry):
            one(k).start()
            return carry

        lax.fori_loop(1, n, body, 0)

    def landed(sems, n, target):
        rest = target.at[pl.ds(0, n - 1)]
        pltpu.make_async_copy(rest, rest, recv_sem.at[sems]).wait()

    def left(sems, n, target):
        rest = target.at[pl.ds(0, n - 1)]
        pltpu.make_async_copy(rest, rest, send_sem.at[sems]).wait()

    tiles = hd // 128
    for i in range(rank // 8):
        for j in range(tiles):
            part_p[i * tiles + j] = part[i * 8 : i * 8 + 8, j * 128 : j * 128 + 128]
    plane_p[dp] = part_p[dp]
    exchange("dp", nd, dp, 0, lambda there: part_p.at[there], plane_p)
    landed(0, nd, plane_p)
    deep_p[z] = jnp.sum(plane_p[...], axis=0)
    exchange("tensor", nz, z, 1, lambda there: deep_p.at[z], deep_p)
    landed(1, nz, deep_p)
    full_p[dp] = jnp.sum(deep_p[...], axis=0)
    exchange("dp", nd, dp, 2, lambda there: full_p.at[dp], full_p)
    landed(2, nd, full_p)
    pt = jnp.concatenate(
        [
            jnp.concatenate([full_p[i * tiles + j] for j in range(tiles)], axis=1)
            for i in range(rank // 8)
        ],
        axis=0,
    )

    ut = dot3(pt, merged[...].reshape(hd, width), NN)
    urows = part_u.shape[1]
    utiles = width // 128
    for i in range(rank // urows):
        for j in range(utiles):
            part_u[i * utiles + j] = ut[i * urows : (i + 1) * urows, j * 128 : j * 128 + 128]
    plane_u[dp] = part_u[dp]
    exchange("dp", nd, dp, 3, lambda there: part_u.at[there], plane_u)

    gram = lax.dot_general(pt, pt, NT, precision=HIGHEST, preferred_element_type=F32)
    row_id = lax.broadcasted_iota(jnp.int32, (rank, 1), 0)
    eye = (
        lax.broadcasted_iota(jnp.int32, (rank, rank), 0)
        == lax.broadcasted_iota(jnp.int32, (rank, rank), 1)
    ).astype(F32)
    x = jnp.concatenate([gram, eye], axis=1)

    def eliminate(x, start, stop):
        for k in range(start, stop):
            d = x[k : k + 1, k : k + 1]
            r = lax.rsqrt(d)
            r = r * (1.5 - 0.5 * d * r * r)
            row = x[k : k + 1, :] * r
            column = x[:, k : k + 1] * r
            x = jnp.where(row_id == k, row, jnp.where(row_id > k, x - column * row, x))
        return x

    x = eliminate(x, 0, rank // 2)
    landed(3, nd, plane_u)
    full_u[dp] = jnp.sum(plane_u[...], axis=0)
    exchange("dp", nd, dp, 4, lambda there: full_u.at[dp], full_u)
    x = eliminate(x, rank // 2, rank)
    inverse = x[:, rank:]
    landed(4, nd, full_u)
    ut = jnp.concatenate(
        [
            jnp.concatenate([full_u[i * utiles + j] for j in range(utiles)], axis=1)
            for i in range(rank // urows)
        ],
        axis=0,
    )
    fqt = lax.dot_general(inverse, ut, NN, precision=HIGHEST, preferred_element_type=F32)
    fq[...] = fqt
    fq_store = pltpu.make_async_copy(fq, fq_hbm, store_sem.at[0])
    fq_store.start()
    mix = lax.dot_general(inverse, fqt, TN, precision=HIGHEST, preferred_element_type=F32) / nd
    p1, p2 = split2(pt)
    m1, m2 = split2(mix)
    left_side = jnp.concatenate([p1, p1, p2], axis=0)
    right_side = jnp.concatenate([m1, m2, m1], axis=0)
    stores = []
    groups = 4
    per = nz // groups
    for g in range(groups):
        n = per * hb
        low = lax.dot_general(
            left_side[:, g * n : (g + 1) * n], right_side, TN, preferred_element_type=F32
        )
        at = pl.ds(g * per, per)
        out[at] = (merged[at] - low.reshape(per, hb, width)).astype(BF16)
        store = pltpu.make_async_copy(out.at[at], new_hbm.at[at], store_sem.at[1 + g])
        store.start()
        stores.append(store)

    def sent(s, carry):
        for piece in range(PIECES):
            for way in range(2):
                ring(way, s, piece).wait_send()
        return carry

    lax.fori_loop(0, half - 1, sent, 0)
    for piece in range(PIECES):
        ring(0 if piece < PIECES // 2 else 1, half - 1, piece).wait_send()
    left(0, nd, plane_p)
    left(1, nz, deep_p)
    left(2, nd, full_p)
    left(3, nd, plane_u)
    left(4, nd, full_u)
    fq_store.wait()
    for store in stores:
        store.wait()


def local(nd, nz, tokens, grad_out, error_old, power_q):
    tok_n, hb = grad_out.shape
    width = tokens.shape[1]
    rank = power_q.shape[1]
    hd = hb * nz
    chunk = rank * hd // nd // 128
    urows = rank * width // nd // 128
    operands = (grad_out.T, tokens, error_old.reshape(nz, hb, width), power_q.T)
    any_space = pl.BlockSpec(memory_space=pl.ANY)
    fqt, new = pl.pallas_call(
        functools.partial(kernel, nd, nz),
        out_shape=(
            jax.ShapeDtypeStruct((rank, width), F32),
            jax.ShapeDtypeStruct((nz, hb, width), BF16),
        ),
        in_specs=[any_space] * 4,
        out_specs=(any_space, any_space),
        scratch_shapes=[
            pltpu.VMEM((nz, hb, tok_n), BF16),
            pltpu.VMEM((tok_n, width), BF16),
            pltpu.VMEM((nz, hb, width), BF16),
            pltpu.VMEM((rank, width), F32),
            pltpu.VMEM((nz, hb, width), F32),
            pltpu.VMEM((nz, hb, width), BF16),
            pltpu.VMEM((rank, width), F32),
            pltpu.VMEM((nd, chunk, 128), F32),
            pltpu.VMEM((nd, chunk, 128), F32),
            pltpu.VMEM((nz, chunk, 128), F32),
            pltpu.VMEM((nd, chunk, 128), F32),
            pltpu.VMEM((nd, urows, 128), F32),
            pltpu.VMEM((nd, urows, 128), F32),
            pltpu.VMEM((nd, urows, 128), F32),
            pltpu.SemaphoreType.DMA((4,)),
            pltpu.SemaphoreType.DMA((2, nz // 2, PIECES)),
            pltpu.SemaphoreType.DMA((2, nz // 2, PIECES)),
            pltpu.SemaphoreType.DMA((5,)),
            pltpu.SemaphoreType.DMA((5,)),
            pltpu.SemaphoreType.DMA((5,)),
        ],
        compiler_params=pltpu.CompilerParams(
            collective_id=0, has_side_effects=True, vmem_limit_bytes=48 * 1024 * 1024
        ),
    )(*(pltpu.with_memory_space_constraint(a, pltpu.HBM) for a in operands))
    return fqt.T, new.reshape(1, hd, width)


def solution(mesh):
    placed = (P("dp", "tensor"), P("dp", "tensor"), P("dp", None, "tensor"), P("tensor", None))
    return jax.shard_map(
        functools.partial(local, mesh.shape["dp"], mesh.shape["tensor"]),
        mesh=mesh,
        in_specs=placed,
        out_specs=(P("tensor", None), P("dp", None, "tensor")),
        check_vma=False,
    )
```

```python
import functools
import math

import jax
import jax.numpy as jnp
from jax import lax
from jax.experimental import pallas as pl
from jax.experimental.pallas import tpu as pltpu
from jax.sharding import PartitionSpec as P

F32 = jnp.float32
BF16 = jnp.bfloat16
MESH = pl.DeviceIdType.MESH
HIGHEST = lax.Precision.HIGHEST
NT = (((1,), (1,)), ((), ()))
NN = (((1,), (0,)), ((), ()))
TN = (((0,), (0,)), ((), ()))
PIECES = 4
BATCHES = 8


def split2(x):
    hi = x.astype(BF16)
    return hi, (x - hi.astype(F32)).astype(BF16)


def dot3(a, b, dims):
    a1, a2 = split2(a)
    b1, b2 = split2(b)
    dot = functools.partial(lax.dot_general, dimension_numbers=dims, preferred_element_type=F32)
    return dot(a1, b1) + (dot(a1, b2) + dot(a2, b1))


def kernel(
    nd, nz, gt_hbm, tok_hbm, err_hbm, qt_hbm, fq_hbm, new_hbm,
    gt, tok, err, qt, merged, out, fq,
    stage, plane_m, total_m, late_stage, late_plane, deep_p, full_p, natural_p,
    part_u, plane_u, full_u,
    load_sem, ring_send, ring_recv, send_sem, recv_sem, store_sem,
):
    dp = lax.axis_index("dp")
    z = lax.axis_index("tensor")
    hb = gt.shape[1]
    rows = hb // PIECES
    half = nz // 2
    rank, width = qt.shape
    q = qt
    own = hb // nd
    across = math.isqrt(nd // 2)
    place = (dp // (2 * across), lax.rem(dp // 2, across), lax.rem(dp, 2))
    offsets = [(i, j, k) for i in range(across) for j in range(across) for k in range(2)][1:]
    far_first = sorted(offsets, key=lambda o: -sum(min(v, across - v) for v in o[:2]))

    loads = [
        pltpu.make_async_copy(gt_hbm, gt.at[z], load_sem.at[0]),
        pltpu.make_async_copy(tok_hbm, tok, load_sem.at[1]),
        pltpu.make_async_copy(err_hbm, err, load_sem.at[2]),
        pltpu.make_async_copy(qt_hbm, qt, load_sem.at[3]),
    ]
    for load in loads:
        load.start()

    barrier = pltpu.get_barrier_semaphore()

    def greet(axis, n, me):
        def body(k, carry):
            pl.semaphore_signal(
                barrier, inc=1, device_id={axis: lax.rem(me + k, n)}, device_id_type=MESH
            )
            return carry

        lax.fori_loop(1, n, body, 0)

    for step in (1, nz - 1):
        pl.semaphore_signal(
            barrier, inc=1, device_id={"tensor": lax.rem(z + step, nz)}, device_id_type=MESH
        )
    greet("dp", nd, dp)
    pl.semaphore_wait(barrier, nd + 1)

    def ring(way, step, piece):
        sign = 1 if way == 0 else -1
        block = lax.rem(z - sign * step + 2 * nz, nz)
        there = lax.rem(z + sign + nz, nz)
        ref = gt.at[block, pl.ds(piece * rows, rows)]
        return pltpu.make_async_remote_copy(
            src_ref=ref,
            dst_ref=ref,
            send_sem=ring_send.at[way, step, piece],
            recv_sem=ring_recv.at[way, step, piece],
            device_id={"tensor": there},
            device_id_type=MESH,
        )

    def arrived(way, step, piece):
        sign = 1 if way == 0 else -1
        block = lax.rem(z - sign * (step + 1) + 2 * nz, nz)
        ref = gt.at[block, pl.ds(piece * rows, rows)]
        pltpu.make_async_copy(ref, ref, ring_recv.at[way, step, piece]).wait()

    def exchange_dp(sems, source, target):
        for offset in far_first:
            there = (
                lax.rem(place[0] + offset[0], across) * across
                + lax.rem(place[1] + offset[1], across)
            ) * 2 + lax.rem(place[2] + offset[2], 2)
            pltpu.make_async_remote_copy(
                src_ref=source(there),
                dst_ref=target.at[dp],
                send_sem=send_sem.at[sems],
                recv_sem=recv_sem.at[sems],
                device_id={"dp": there},
                device_id_type=MESH,
            ).start()

    def exchange_z(sems, source, target):
        for offset in sorted(range(1, nz), key=lambda k: -min(k, nz - k)):
            pltpu.make_async_remote_copy(
                src_ref=source,
                dst_ref=target.at[z],
                send_sem=send_sem.at[sems],
                recv_sem=recv_sem.at[sems],
                device_id={"tensor": lax.rem(z + offset, nz)},
                device_id_type=MESH,
            ).start()

    def landed(sems, n, target):
        rest = target.at[pl.ds(0, n - 1)]
        pltpu.make_async_copy(rest, rest, recv_sem.at[sems]).wait()

    def left(sems, n, target):
        rest = target.at[pl.ds(0, n - 1)]
        pltpu.make_async_copy(rest, rest, send_sem.at[sems]).wait()

    def at(offset):
        return lax.rem(z + offset + 2 * nz, nz)

    def multiply(*blocks):
        x = [gt[block] for block in blocks]
        x = x[0] if len(x) == 1 else jnp.concatenate(x, axis=0)
        y = jnp.dot(x, tok[...], preferred_element_type=F32)
        parts = []
        for i, block in enumerate(blocks):
            part = y[i * hb : (i + 1) * hb] + err[block].astype(F32)
            merged[block] = part
            parts.append(part.reshape(nd, own, width))
        return parts

    def batch_of(step):
        return step * BATCHES // half

    slots = {}
    for step in range(half):
        for block in ((0,) if step == 0 else (step, -step)):
            batch = batch_of(step)
            slots[block] = (batch, sum(1 for b in slots.values() if b[0] == batch))
    counts = [sum(1 for b in slots.values() if b[0] == k) for k in range(BATCHES)]
    starts = [sum(counts[:k]) for k in range(BATCHES)]

    def put(step):
        blocks = (0,) if step == 0 else (step, -step)
        for block, part in zip(blocks, multiply(*(at(b) for b in blocks)), strict=True):
            batch, slot = slots[block]
            stage[:, starts[batch] + slot] = part
        batch = batch_of(step)
        if step == half - 1 or batch_of(step + 1) != batch:
            span = pl.ds(starts[batch], counts[batch])
            plane_m[dp, span] = stage[dp, span]
            for offset in far_first:
                there = (
                    lax.rem(place[0] + offset[0], across) * across
                    + lax.rem(place[1] + offset[1], across)
                ) * 2 + lax.rem(place[2] + offset[2], 2)
                pltpu.make_async_remote_copy(
                    src_ref=stage.at[there, span],
                    dst_ref=plane_m.at[dp, span],
                    send_sem=send_sem.at[5 + batch],
                    recv_sem=recv_sem.at[5 + batch],
                    device_id={"dp": there},
                    device_id_type=MESH,
                ).start()

    def gather_batch(batch):
        span = pl.ds(starts[batch], counts[batch])
        rest = plane_m.at[pl.ds(0, nd - 1), span]
        pltpu.make_async_copy(rest, rest, recv_sem.at[5 + batch]).wait()
        for block, (b, slot) in slots.items():
            if b == batch:
                total_m[at(block)] = jnp.sum(plane_m[:, starts[b] + slot], axis=0)

    loads[0].wait()
    for piece in range(PIECES):
        ring(0, 0, piece).start()
        ring(1, 0, piece).start()
    for load in loads[1:]:
        load.wait()
    put(0)
    for s in range(1, half):
        for piece in range(PIECES):
            for way in range(2):
                arrived(way, s - 1, piece)
                if s < half - 1 or (piece < PIECES // 2) == (way == 0):
                    ring(way, s, piece).start()
        put(s)
        if s < half - 1 and batch_of(s + 1) != batch_of(s) and batch_of(s) > 0:
            gather_batch(batch_of(s) - 1)
    gather_batch(BATCHES - 2)
    for piece in range(PIECES):
        arrived(0 if piece < PIECES // 2 else 1, half - 1, piece)
    late_stage[...] = multiply(at(half))[0]
    late_plane[dp] = late_stage[dp]
    exchange_dp(0, lambda there: late_stage.at[there], late_plane)
    gather_batch(BATCHES - 1)
    landed(0, nd, late_plane)
    total_m[at(half)] = jnp.sum(late_plane[...], axis=0)

    hd = nz * hb
    rows_p = nz * own
    m = total_m[...].reshape(rows_p, width)
    part = dot3(m, q[...], NT)
    groups = 128 // rank
    high = rows_p // groups
    deep_p[z] = jnp.concatenate([part[k * high : (k + 1) * high] for k in range(groups)], axis=1)
    exchange_z(1, deep_p.at[z], deep_p)
    landed(1, nz, deep_p)
    packed = jnp.sum(deep_p[...], axis=0)

    def unpack(x):
        return jnp.concatenate([x[:, k * rank : (k + 1) * rank] for k in range(groups)], axis=0)

    full_p[dp] = packed
    exchange_dp(2, lambda there: full_p.at[dp], full_p)

    ut = dot3(unpack(packed), m, TN)
    urows = part_u.shape[1]
    utiles = width // 128
    for i in range(rank // urows):
        for j in range(utiles):
            part_u[i * utiles + j] = ut[i * urows : (i + 1) * urows, j * 128 : j * 128 + 128]
    plane_u[dp] = part_u[dp]
    exchange_dp(3, lambda there: part_u.at[there], plane_u)
    landed(2, nd, full_p)
    for j in range(nd):
        natural_p[:, j * own : (j + 1) * own] = unpack(full_p[j]).reshape(nz, own, rank)
    p = natural_p[...].reshape(hd, rank)

    gram = lax.dot_general(p, p, TN, precision=HIGHEST, preferred_element_type=F32)
    row_id = lax.broadcasted_iota(jnp.int32, (rank, 1), 0)
    eye = (
        lax.broadcasted_iota(jnp.int32, (rank, rank), 0)
        == lax.broadcasted_iota(jnp.int32, (rank, rank), 1)
    ).astype(F32)
    x = jnp.concatenate([gram, eye], axis=1)

    def eliminate(x, start, stop):
        for k in range(start, stop):
            d = x[k : k + 1, k : k + 1]
            r = lax.rsqrt(d)
            r = r * (1.5 - 0.5 * d * r * r)
            row = x[k : k + 1, :] * r
            column = x[:, k : k + 1] * r
            x = jnp.where(row_id == k, row, jnp.where(row_id > k, x - column * row, x))
        return x

    landed(3, nd, plane_u)
    full_u[dp] = jnp.sum(plane_u[...], axis=0)
    exchange_dp(4, lambda there: full_u.at[dp], full_u)
    x = eliminate(x, 0, rank)
    inverse = x[:, rank:]
    landed(4, nd, full_u)
    ut = jnp.concatenate(
        [
            jnp.concatenate([full_u[i * utiles + j] for j in range(utiles)], axis=1)
            for i in range(rank // urows)
        ],
        axis=0,
    )
    fqt = lax.dot_general(inverse, ut, NN, precision=HIGHEST, preferred_element_type=F32)
    fq[...] = fqt
    fq_store = pltpu.make_async_copy(fq, fq_hbm, store_sem.at[0])
    fq_store.start()
    mix = lax.dot_general(inverse, fqt, TN, precision=HIGHEST, preferred_element_type=F32) / nd
    p1, p2 = split2(p)
    m1, m2 = split2(mix)
    left_side = jnp.concatenate([p1, p1, p2], axis=1)
    right_side = jnp.concatenate([m1, m2, m1], axis=0)
    stores = []
    parts = 4
    per = nz // parts
    for g in range(parts):
        n = per * hb
        low = lax.dot_general(
            left_side[g * n : (g + 1) * n], right_side, NN, preferred_element_type=F32
        )
        at = pl.ds(g * per, per)
        out[at] = (merged[at] - low.reshape(per, hb, width)).astype(BF16)
        store = pltpu.make_async_copy(out.at[at], new_hbm.at[at], store_sem.at[1 + g])
        store.start()
        stores.append(store)

    def sent(s, carry):
        for piece in range(PIECES):
            for way in range(2):
                ring(way, s, piece).wait_send()
        return carry

    lax.fori_loop(0, half - 1, sent, 0)
    for piece in range(PIECES):
        ring(0 if piece < PIECES // 2 else 1, half - 1, piece).wait_send()
    for batch in range(BATCHES):
        rest = plane_m.at[pl.ds(0, nd - 1), pl.ds(starts[batch], counts[batch])]
        pltpu.make_async_copy(rest, rest, send_sem.at[5 + batch]).wait()
    left(0, nd, late_plane)
    left(1, nz, deep_p)
    left(2, nd, full_p)
    left(3, nd, plane_u)
    left(4, nd, full_u)
    fq_store.wait()
    for store in stores:
        store.wait()


def local(nd, nz, tokens, grad_out, error_old, power_q):
    tok_n, hb = grad_out.shape
    width = tokens.shape[1]
    rank = power_q.shape[1]
    hd = hb * nz
    chunk = rank * hd // nd // 128
    urows = rank * width // nd // 128
    operands = (grad_out.T, tokens, error_old.reshape(nz, hb, width), power_q.T)
    any_space = pl.BlockSpec(memory_space=pl.ANY)
    fqt, new = pl.pallas_call(
        functools.partial(kernel, nd, nz),
        out_shape=(
            jax.ShapeDtypeStruct((rank, width), F32),
            jax.ShapeDtypeStruct((nz, hb, width), BF16),
        ),
        in_specs=[any_space] * 4,
        out_specs=(any_space, any_space),
        scratch_shapes=[
            pltpu.VMEM((nz, hb, tok_n), BF16),
            pltpu.VMEM((tok_n, width), BF16),
            pltpu.VMEM((nz, hb, width), BF16),
            pltpu.VMEM((rank, width), F32),
            pltpu.VMEM((nz, hb, width), F32),
            pltpu.VMEM((nz, hb, width), BF16),
            pltpu.VMEM((rank, width), F32),
            pltpu.VMEM((nd, nz - 1, hb // nd, width), F32),
            pltpu.VMEM((nd, nz - 1, hb // nd, width), F32),
            pltpu.VMEM((nz, hb // nd, width), F32),
            pltpu.VMEM((nd, hb // nd, width), F32),
            pltpu.VMEM((nd, hb // nd, width), F32),
            pltpu.VMEM((nz, chunk, 128), F32),
            pltpu.VMEM((nd, chunk, 128), F32),
            pltpu.VMEM((nz, hb, rank), F32),
            pltpu.VMEM((nd, urows, 128), F32),
            pltpu.VMEM((nd, urows, 128), F32),
            pltpu.VMEM((nd, urows, 128), F32),
            pltpu.SemaphoreType.DMA((4,)),
            pltpu.SemaphoreType.DMA((2, nz // 2, PIECES)),
            pltpu.SemaphoreType.DMA((2, nz // 2, PIECES)),
            pltpu.SemaphoreType.DMA((5 + BATCHES,)),
            pltpu.SemaphoreType.DMA((5 + BATCHES,)),
            pltpu.SemaphoreType.DMA((5,)),
        ],
        compiler_params=pltpu.CompilerParams(
            collective_id=0, has_side_effects=True, vmem_limit_bytes=48 * 1024 * 1024
        ),
    )(*(pltpu.with_memory_space_constraint(a, pltpu.HBM) for a in operands))
    return fqt.T, new.reshape(1, hd, width)


def solution(mesh):
    placed = (P("dp", "tensor"), P("dp", "tensor"), P("dp", None, "tensor"), P("tensor", None))
    return jax.shard_map(
        functools.partial(local, mesh.shape["dp"], mesh.shape["tensor"]),
        mesh=mesh,
        in_specs=placed,
        out_specs=(P("tensor", None), P("dp", None, "tensor")),
        check_vma=False,
    )
```

```python
import functools
import math

import jax
import jax.numpy as jnp
from jax import lax
from jax.experimental import pallas as pl
from jax.experimental.pallas import tpu as pltpu
from jax.sharding import PartitionSpec as P

F32 = jnp.float32
BF16 = jnp.bfloat16
MESH = pl.DeviceIdType.MESH
HIGHEST = lax.Precision.HIGHEST
GROUPS = 4
NT = (((1,), (1,)), ((), ()))
NN = (((1,), (0,)), ((), ()))
TN = (((0,), (0,)), ((), ()))
PIECES = 4


def split2(x):
    hi = x.astype(BF16)
    return hi, (x - hi.astype(F32)).astype(BF16)


def dot3(a, b, dims):
    a1, a2 = split2(a)
    b1, b2 = split2(b)
    dot = functools.partial(lax.dot_general, dimension_numbers=dims, preferred_element_type=F32)
    return dot(a1, b1) + (dot(a1, b2) + dot(a2, b1))


def kernel(
    nd, nz, gt_hbm, tok_hbm, err_hbm, qt_hbm, fq, merged, left_side, right_side,
    gt, tok, err, qt,
    stage, plane_m, total_m, late_stage, late_plane, deep_p, late_p, full_p, natural_p,
    part_u, plane_u, full_u,
    load_sem, ring_send, ring_recv, send_sem, recv_sem,
):
    dp = lax.axis_index("dp")
    z = lax.axis_index("tensor")
    hb = gt.shape[1]
    rows = hb // PIECES
    half = nz // 2
    rank, width = qt.shape
    q = qt
    own = hb // nd
    across = math.isqrt(nd // 2)
    place = (dp // (2 * across), lax.rem(dp // 2, across), lax.rem(dp, 2))
    offsets = [(i, j, k) for i in range(across) for j in range(across) for k in range(2)][1:]
    far_first = sorted(offsets, key=lambda o: -sum(min(v, across - v) for v in o[:2]))

    loads = [
        pltpu.make_async_copy(gt_hbm, gt.at[z], load_sem.at[0]),
        pltpu.make_async_copy(tok_hbm, tok, load_sem.at[1]),
        pltpu.make_async_copy(err_hbm, err, load_sem.at[2]),
        pltpu.make_async_copy(qt_hbm, qt, load_sem.at[3]),
    ]
    for load in loads:
        load.start()

    barrier = pltpu.get_barrier_semaphore()

    def greet(axis, n, me):
        def body(k, carry):
            pl.semaphore_signal(
                barrier, inc=1, device_id={axis: lax.rem(me + k, n)}, device_id_type=MESH
            )
            return carry

        lax.fori_loop(1, n, body, 0)

    for step in (1, nz - 1):
        pl.semaphore_signal(
            barrier, inc=1, device_id={"tensor": lax.rem(z + step, nz)}, device_id_type=MESH
        )
    greet("dp", nd, dp)
    pl.semaphore_wait(barrier, nd + 1)

    def ring(way, step, piece):
        sign = 1 if way == 0 else -1
        block = lax.rem(z - sign * step + 2 * nz, nz)
        there = lax.rem(z + sign + nz, nz)
        ref = gt.at[block, pl.ds(piece * rows, rows)]
        return pltpu.make_async_remote_copy(
            src_ref=ref,
            dst_ref=ref,
            send_sem=ring_send.at[way, step, piece],
            recv_sem=ring_recv.at[way, step, piece],
            device_id={"tensor": there},
            device_id_type=MESH,
        )

    def arrived(way, step, piece):
        sign = 1 if way == 0 else -1
        block = lax.rem(z - sign * (step + 1) + 2 * nz, nz)
        ref = gt.at[block, pl.ds(piece * rows, rows)]
        pltpu.make_async_copy(ref, ref, ring_recv.at[way, step, piece]).wait()

    def exchange_dp(sems, source, target):
        for offset in far_first:
            there = (
                lax.rem(place[0] + offset[0], across) * across
                + lax.rem(place[1] + offset[1], across)
            ) * 2 + lax.rem(place[2] + offset[2], 2)
            pltpu.make_async_remote_copy(
                src_ref=source(there),
                dst_ref=target.at[dp],
                send_sem=send_sem.at[sems],
                recv_sem=recv_sem.at[sems],
                device_id={"dp": there},
                device_id_type=MESH,
            ).start()

    def exchange_z(sems, source, target):
        for offset in sorted(range(1, nz), key=lambda k: -min(k, nz - k)):
            pltpu.make_async_remote_copy(
                src_ref=source,
                dst_ref=target.at[z],
                send_sem=send_sem.at[sems],
                recv_sem=recv_sem.at[sems],
                device_id={"tensor": lax.rem(z + offset, nz)},
                device_id_type=MESH,
            ).start()

    def landed(sems, n, target):
        rest = target.at[pl.ds(0, n - 1)]
        pltpu.make_async_copy(rest, rest, recv_sem.at[sems]).wait()

    def left(sems, n, target):
        rest = target.at[pl.ds(0, n - 1)]
        pltpu.make_async_copy(rest, rest, send_sem.at[sems]).wait()

    def at(offset):
        return lax.rem(z + offset + 2 * nz, nz)

    def multiply(*blocks):
        x = [gt[block] for block in blocks]
        x = x[0] if len(x) == 1 else jnp.concatenate(x, axis=0)
        y = jnp.dot(x, tok[...], preferred_element_type=F32)
        parts = []
        for i, block in enumerate(blocks):
            part = y[i * hb : (i + 1) * hb] + err[block].astype(F32)
            merged[block] = part
            parts.append(part.reshape(nd, own, width))
        return parts

    slots = {}
    for step in range(half):
        for block in ((0,) if step == 0 else (step, -step)):
            batch = step
            slots[block] = (batch, sum(1 for b in slots.values() if b[0] == batch))
    counts = [sum(1 for b in slots.values() if b[0] == k) for k in range(half)]
    starts = [sum(counts[:k]) for k in range(half)]

    pending = []

    def send_rows(batch, span, offset):
        there = (
            lax.rem(place[0] + offset[0], across) * across
            + lax.rem(place[1] + offset[1], across)
        ) * 2 + lax.rem(place[2] + offset[2], 2)
        pltpu.make_async_remote_copy(
            src_ref=stage.at[there, span],
            dst_ref=plane_m.at[dp, span],
            send_sem=send_sem.at[5 + batch],
            recv_sem=recv_sem.at[5 + batch],
            device_id={"dp": there},
            device_id_type=MESH,
        ).start()

    def send_pending(n):
        for _ in range(min(n, len(pending))):
            pending.pop(0)()

    def put(step):
        blocks = (0,) if step == 0 else (step, -step)
        for block, part in zip(blocks, multiply(*(at(b) for b in blocks)), strict=True):
            batch, slot = slots[block]
            stage[:, starts[batch] + slot] = part
        batch = step
        if True:
            span = pl.ds(starts[batch], counts[batch])
            plane_m[dp, span] = stage[dp, span]
            for offset in far_first:
                pending.append(functools.partial(send_rows, batch, span, offset))
            if step == half - 1:
                send_pending(len(pending))

    def gather_batch(batch):
        span = pl.ds(starts[batch], counts[batch])
        rest = plane_m.at[pl.ds(0, nd - 1), span]
        pltpu.make_async_copy(rest, rest, recv_sem.at[5 + batch]).wait()
        for block, (b, slot) in slots.items():
            if b == batch:
                total_m[at(block)] = jnp.sum(plane_m[:, starts[b] + slot], axis=0)

    loads[0].wait()
    for piece in range(PIECES):
        ring(0, 0, piece).start()
        ring(1, 0, piece).start()
    for load in loads[1:]:
        load.wait()
    put(0)
    for s in range(1, half):
        for piece in range(PIECES):
            for way in range(2):
                arrived(way, s - 1, piece)
                if s < half - 1 or (piece < PIECES // 2) == (way == 0):
                    ring(way, s, piece).start()
            send_pending(nd // PIECES if piece < PIECES - 1 else nd)
        put(s)
        if s > 1:
            gather_batch(s - 2)
    gather_batch(half - 2)
    for piece in range(PIECES):
        arrived(0 if piece < PIECES // 2 else 1, half - 1, piece)
    late_stage[...] = multiply(at(half))[0]
    late_plane[dp] = late_stage[dp]
    exchange_dp(0, lambda there: late_stage.at[there], late_plane)

    hd = nz * hb
    rows_p = nz * own
    groups = 128 // rank
    high = rows_p // groups
    late_blocks = (half - 1, 1 - half, half)
    for block in late_blocks:
        total_m[at(block)] = jnp.zeros((own, width), F32)

    def pack(x):
        return jnp.concatenate([x[k * high : (k + 1) * high] for k in range(groups)], axis=1)

    def unpack(x):
        return jnp.concatenate([x[:, k * rank : (k + 1) * rank] for k in range(groups)], axis=0)

    deep_p[z] = pack(dot3(total_m[...].reshape(rows_p, width), q[...], NT))
    exchange_z(1, deep_p.at[z], deep_p)
    gather_batch(half - 1)
    landed(0, nd, late_plane)
    total_m[at(half)] = jnp.sum(late_plane[...], axis=0)
    late = jnp.concatenate([total_m[at(block)] for block in late_blocks], axis=0)
    late = dot3(late, q[...], NT)
    late = [late[k * own : (k + 1) * own] for k in range(3)] + [jnp.zeros((own, 128 - 3 * rank), F32)]
    late_p[z] = jnp.concatenate(late, axis=1)
    exchange_z(5 + half, late_p.at[z], late_p)
    m = total_m[...].reshape(rows_p, width)
    landed(1, nz, deep_p)
    early = unpack(jnp.sum(deep_p[...], axis=0))
    landed(5 + half, nz, late_p)
    mine = early
    for k, block in enumerate(late_blocks):
        x = late_p[...][:, :, k * rank : (k + 1) * rank]
        shift = -block % nz
        x = jnp.concatenate([x[shift:], x[:shift]], axis=0)
        mine = mine + x.reshape(rows_p, rank)
    packed = pack(mine)
    full_p[dp] = packed

    ut = dot3(mine, m, TN)
    urows = part_u.shape[1]
    utiles = width // 128
    for i in range(rank // urows):
        for j in range(utiles):
            part_u[i * utiles + j] = ut[i * urows : (i + 1) * urows, j * 128 : j * 128 + 128]
    plane_u[dp] = part_u[dp]
    exchange_dp(3, lambda there: part_u.at[there], plane_u)
    exchange_dp(2, lambda there: full_p.at[dp], full_p)
    landed(3, nd, plane_u)
    full_u[dp] = jnp.sum(plane_u[...], axis=0)
    exchange_dp(4, lambda there: full_u.at[dp], full_u)
    landed(2, nd, full_p)
    for j in range(nd):
        natural_p[:, j * own : (j + 1) * own] = unpack(full_p[j]).reshape(nz, own, rank)
    p = natural_p[...].reshape(hd, rank)

    gram = lax.dot_general(p, p, TN, precision=HIGHEST, preferred_element_type=F32)
    row_id = lax.broadcasted_iota(jnp.int32, (rank, 1), 0)
    eye = (
        lax.broadcasted_iota(jnp.int32, (rank, rank), 0)
        == lax.broadcasted_iota(jnp.int32, (rank, rank), 1)
    ).astype(F32)
    x = jnp.concatenate([gram, eye], axis=1)

    def eliminate(x, start, stop):
        for k in range(start, stop):
            d = x[k : k + 1, k : k + 1]
            r = lax.rsqrt(d)
            r = r * (1.5 - 0.5 * d * r * r)
            row = x[k : k + 1, :] * r
            column = x[:, k : k + 1] * r
            x = jnp.where(row_id == k, row, jnp.where(row_id > k, x - column * row, x))
        return x

    x = eliminate(x, 0, rank)
    inverse = x[:, rank:]
    square = lax.dot_general(inverse, inverse, TN, precision=HIGHEST, preferred_element_type=F32)
    joint = jnp.concatenate([inverse, square / nd], axis=0)
    p1, p2 = split2(p)
    left_side[...] = jnp.concatenate([p1, p1, p2], axis=1)
    def sent(s, carry):
        for piece in range(PIECES):
            for way in range(2):
                ring(way, s, piece).wait_send()
        return carry

    lax.fori_loop(0, half - 1, sent, 0)
    for piece in range(PIECES):
        ring(0 if piece < PIECES // 2 else 1, half - 1, piece).wait_send()
    for batch in range(half):
        rest = plane_m.at[pl.ds(0, nd - 1), pl.ds(starts[batch], counts[batch])]
        pltpu.make_async_copy(rest, rest, send_sem.at[5 + batch]).wait()
    left(0, nd, late_plane)
    left(1, nz, deep_p)
    left(5 + half, nz, late_p)
    left(2, nd, full_p)
    left(3, nd, plane_u)
    landed(4, nd, full_u)
    ut = jnp.concatenate(
        [
            jnp.concatenate([full_u[i * utiles + j] for j in range(utiles)], axis=1)
            for i in range(rank // urows)
        ],
        axis=0,
    )
    both = lax.dot_general(joint, ut, NN, precision=HIGHEST, preferred_element_type=F32)
    fqt = both[:rank]
    fq[...] = fqt
    m1, m2 = split2(both[rank:])
    right_side[...] = jnp.concatenate([m1, m2, m1], axis=0)
    left(4, nd, full_u)


def finish(fq, merged, left_side, right_side, fq_hbm, new_hbm, out, store_sem):
    nz, hb, width = out.shape
    stores = [pltpu.make_async_copy(fq, fq_hbm, store_sem.at[0])]
    stores[0].start()
    per = nz // GROUPS
    for g in range(GROUPS):
        low = jnp.dot(
            left_side[g * per * hb : (g + 1) * per * hb],
            right_side[...],
            preferred_element_type=F32,
        )
        span = pl.ds(g * per, per)
        out[span] = (merged[span] - low.reshape(per, hb, width)).astype(BF16)
        stores.append(pltpu.make_async_copy(out.at[span], new_hbm.at[span], store_sem.at[1 + g]))
        stores[-1].start()
    for store in stores:
        store.wait()


def local(nd, nz, tokens, grad_out, error_old, power_q):
    tok_n, hb = grad_out.shape
    width = tokens.shape[1]
    rank = power_q.shape[1]
    hd = hb * nz
    chunk = rank * hd // nd // 128
    urows = rank * width // nd // 128
    operands = (grad_out.T, tokens, error_old.reshape(nz, hb, width), power_q.T)
    any_space = pl.BlockSpec(memory_space=pl.ANY)
    held = pl.pallas_call(
        functools.partial(kernel, nd, nz),
        out_shape=(
            pltpu.VMEM((rank, width), F32),
            pltpu.VMEM((nz, hb, width), F32),
            pltpu.VMEM((hd, 3 * rank), BF16),
            pltpu.VMEM((3 * rank, width), BF16),
        ),
        in_specs=[any_space] * 4,
        out_specs=(pl.BlockSpec(memory_space=pltpu.VMEM),) * 4,
        scratch_shapes=[
            pltpu.VMEM((nz, hb, tok_n), BF16),
            pltpu.VMEM((tok_n, width), BF16),
            pltpu.VMEM((nz, hb, width), BF16),
            pltpu.VMEM((rank, width), F32),
            pltpu.VMEM((nd, nz - 1, hb // nd, width), F32),
            pltpu.VMEM((nd, nz - 1, hb // nd, width), F32),
            pltpu.VMEM((nz, hb // nd, width), F32),
            pltpu.VMEM((nd, hb // nd, width), F32),
            pltpu.VMEM((nd, hb // nd, width), F32),
            pltpu.VMEM((nz, chunk, 128), F32),
            pltpu.VMEM((nz, hb // nd, 128), F32),
            pltpu.VMEM((nd, chunk, 128), F32),
            pltpu.VMEM((nz, hb, rank), F32),
            pltpu.VMEM((nd, urows, 128), F32),
            pltpu.VMEM((nd, urows, 128), F32),
            pltpu.VMEM((nd, urows, 128), F32),
            pltpu.SemaphoreType.DMA((4,)),
            pltpu.SemaphoreType.DMA((2, nz // 2, PIECES)),
            pltpu.SemaphoreType.DMA((2, nz // 2, PIECES)),
            pltpu.SemaphoreType.DMA((6 + nz // 2,)),
            pltpu.SemaphoreType.DMA((6 + nz // 2,)),
        ],
        compiler_params=pltpu.CompilerParams(
            collective_id=0, has_side_effects=True, vmem_limit_bytes=44 * 1024 * 1024
        ),
    )(*(pltpu.with_memory_space_constraint(a, pltpu.HBM) for a in operands))
    fqt, new = pl.pallas_call(
        finish,
        out_shape=(pltpu.HBM((rank, width), F32), pltpu.HBM((nz, hb, width), BF16)),
        in_specs=[pl.BlockSpec(memory_space=pltpu.VMEM)] * 4,
        out_specs=(any_space, any_space),
        scratch_shapes=[
            pltpu.VMEM((nz, hb, width), BF16),
            pltpu.SemaphoreType.DMA((1 + GROUPS,)),
        ],
        compiler_params=pltpu.CompilerParams(vmem_limit_bytes=8 * 1024 * 1024),
    )(*(pltpu.with_memory_space_constraint(a, pltpu.VMEM) for a in held))
    return fqt.T, new.reshape(1, hd, width)


def solution(mesh):
    placed = (P("dp", "tensor"), P("dp", "tensor"), P("dp", None, "tensor"), P("tensor", None))
    return jax.shard_map(
        functools.partial(local, mesh.shape["dp"], mesh.shape["tensor"]),
        mesh=mesh,
        in_specs=placed,
        out_specs=(P("tensor", None), P("dp", None, "tensor")),
        check_vma=False,
    )
```

```python
import functools
import math

import jax
import jax.numpy as jnp
from jax import lax
from jax.experimental import pallas as pl
from jax.experimental.pallas import tpu as pltpu
from jax.sharding import PartitionSpec as P

F32 = jnp.float32
BF16 = jnp.bfloat16
MESH = pl.DeviceIdType.MESH
HIGHEST = lax.Precision.HIGHEST
GROUPS = 4
NT = (((1,), (1,)), ((), ()))
NN = (((1,), (0,)), ((), ()))
TN = (((0,), (0,)), ((), ()))
PIECES = 4


def split2(x):
    hi = x.astype(BF16)
    return hi, (x - hi.astype(F32)).astype(BF16)


def dot3(a, b, dims):
    a1, a2 = split2(a)
    b1, b2 = b if isinstance(b, tuple) else split2(b)
    dot = functools.partial(lax.dot_general, dimension_numbers=dims, preferred_element_type=F32)
    return dot(a1, b1) + (dot(a1, b2) + dot(a2, b1))


def kernel(
    nd, nz, gt_hbm, tok_hbm, err_hbm, qt_hbm, fq, merged, left_side, right_side,
    gt, tok, err, qt,
    stage, plane_m, total_m, late_part, late_land, deep_p, late_p, full_p, natural_p,
    part_u, plane_u, full_u,
    load_sem, ring_send, ring_recv, send_sem, recv_sem,
):
    dp = lax.axis_index("dp")
    z = lax.axis_index("tensor")
    hb = gt.shape[1]
    rows = hb // PIECES
    half = nz // 2
    rank, width = qt.shape
    q = qt
    own = hb // nd
    across = math.isqrt(nd // 2)
    place = (dp // (2 * across), lax.rem(dp // 2, across), lax.rem(dp, 2))
    offsets = [(i, j, k) for i in range(across) for j in range(across) for k in range(2)][1:]
    far_first = sorted(offsets, key=lambda o: -sum(min(v, across - v) for v in o[:2]))

    def peer(offset):
        x, y, core = ((p + o) & (n - 1) for p, o, n in zip(place, offset, (across, across, 2)))
        return (x * across + y) * 2 + core

    loads = [
        pltpu.make_async_copy(gt_hbm, gt.at[z], load_sem.at[0]),
        pltpu.make_async_copy(tok_hbm, tok, load_sem.at[1]),
        pltpu.make_async_copy(err_hbm, err, load_sem.at[2]),
        pltpu.make_async_copy(qt_hbm, qt, load_sem.at[3]),
    ]
    loads[0].start()

    barrier = pltpu.get_barrier_semaphore()
    for step in (1, nz - 1):
        pl.semaphore_signal(
            barrier, inc=1, device_id={"tensor": lax.rem(z + step, nz)}, device_id_type=MESH
        )
    for offset in far_first:
        pl.semaphore_signal(barrier, inc=1, device_id={"dp": peer(offset)}, device_id_type=MESH)
    for load in loads[1:]:
        load.start()
    pl.semaphore_wait(barrier, nd + 1)

    def ring(way, step, piece):
        sign = 1 if way == 0 else -1
        block = lax.rem(z - sign * step + 2 * nz, nz)
        there = lax.rem(z + sign + nz, nz)
        ref = gt.at[block, pl.ds(piece * rows, rows)]
        return pltpu.make_async_remote_copy(
            src_ref=ref,
            dst_ref=ref,
            send_sem=ring_send.at[way, step, piece],
            recv_sem=ring_recv.at[way, step, piece],
            device_id={"tensor": there},
            device_id_type=MESH,
        )

    def arrived(way, step, piece):
        sign = 1 if way == 0 else -1
        block = lax.rem(z - sign * (step + 1) + 2 * nz, nz)
        ref = gt.at[block, pl.ds(piece * rows, rows)]
        pltpu.make_async_copy(ref, ref, ring_recv.at[way, step, piece]).wait()

    def exchange_dp(sems, source, target):
        for offset in far_first:
            there = peer(offset)
            pltpu.make_async_remote_copy(
                src_ref=source(there),
                dst_ref=target.at[dp],
                send_sem=send_sem.at[sems],
                recv_sem=recv_sem.at[sems],
                device_id={"dp": there},
                device_id_type=MESH,
            ).start()

    def exchange_z(sems, source, target):
        for offset in sorted(range(1, nz), key=lambda k: -min(k, nz - k)):
            pltpu.make_async_remote_copy(
                src_ref=source,
                dst_ref=target.at[z],
                send_sem=send_sem.at[sems],
                recv_sem=recv_sem.at[sems],
                device_id={"tensor": lax.rem(z + offset, nz)},
                device_id_type=MESH,
            ).start()

    def landed(sems, n, target):
        rest = target.at[pl.ds(0, n - 1)]
        pltpu.make_async_copy(rest, rest, recv_sem.at[sems]).wait()

    def left(sems, n, target):
        rest = target.at[pl.ds(0, n - 1)]
        pltpu.make_async_copy(rest, rest, send_sem.at[sems]).wait()

    def at(offset):
        return lax.rem(z + offset + 2 * nz, nz)

    def multiply(*blocks):
        x = [gt[block] for block in blocks]
        x = x[0] if len(x) == 1 else jnp.concatenate(x, axis=0)
        y = jnp.dot(x, tok[...], preferred_element_type=F32)
        parts = []
        for i, block in enumerate(blocks):
            part = y[i * hb : (i + 1) * hb] + err[block].astype(F32)
            merged[block] = part
            parts.append(part.reshape(nd, own, width))
        return parts

    slots = {}
    for step in range(half):
        for block in (0,) if step == 0 else (step, -step) + (half,) * (step == half - 1):
            batch = step
            slots[block] = (batch, sum(1 for b in slots.values() if b[0] == batch))
    counts = [sum(1 for b in slots.values() if b[0] == k) for k in range(half)]
    starts = [sum(counts[:k]) for k in range(half)]

    pending = []

    def send_rows(batch, span, offset):
        there = peer(offset)
        pltpu.make_async_remote_copy(
            src_ref=stage.at[there, span],
            dst_ref=plane_m.at[dp, span],
            send_sem=send_sem.at[5 + batch],
            recv_sem=recv_sem.at[5 + batch],
            device_id={"dp": there},
            device_id_type=MESH,
        ).start()

    def send_pending(n):
        for _ in range(min(n, len(pending))):
            pending.pop(0)()

    def put(step):
        blocks = (0,) if step == 0 else (step, -step)
        for block, part in zip(blocks, multiply(*(at(b) for b in blocks)), strict=True):
            batch, slot = slots[block]
            stage[:, starts[batch] + slot] = part
        if step < half - 1:
            span = pl.ds(starts[step], counts[step])
            plane_m[dp, span] = stage[dp, span]
            for offset in far_first:
                pending.append(functools.partial(send_rows, step, span, offset))

    def gather_batch(batch):
        span = pl.ds(starts[batch], counts[batch])
        rest = plane_m.at[pl.ds(0, nd - 1), span]
        pltpu.make_async_copy(rest, rest, recv_sem.at[5 + batch]).wait()
        for block, (b, slot) in slots.items():
            if b == batch:
                total_m[at(block)] = jnp.sum(plane_m[:, starts[b] + slot], axis=0)

    loads[0].wait()
    for piece in range(PIECES):
        ring(0, 0, piece).start()
        ring(1, 0, piece).start()
    for load in loads[1:]:
        load.wait()
    put(0)
    for s in range(1, half):
        for piece in range(PIECES):
            for way in range(2):
                arrived(way, s - 1, piece)
                if s < half - 1 or (piece < PIECES // 2) == (way == 0):
                    ring(way, s, piece).start()
            send_pending(nd // PIECES if piece < PIECES - 1 else nd)
        put(s)
        if s > 1:
            gather_batch(s - 2)
    late_blocks = (half - 1, 1 - half, half)
    q_parts = split2(q[...])
    late = [dot3(merged[at(block)], q_parts, NT) for block in late_blocks[:2]]
    for piece in range(PIECES):
        arrived(0 if piece < PIECES // 2 else 1, half - 1, piece)
    part = multiply(at(half))[0]
    late.append(dot3(merged[at(half)], q_parts, NT))
    late = [x.reshape(nd, own, rank) for x in late] + [jnp.zeros((nd, own, 128 - 3 * rank), F32)]
    late_part[...] = jnp.concatenate(late, axis=2)
    late_land[dp] = late_part[dp]
    exchange_dp(0, lambda there: late_part.at[there], late_land)
    stage[:, starts[half - 1] + 2] = part
    span = pl.ds(starts[half - 1], counts[half - 1])
    plane_m[dp, span] = stage[dp, span]
    for offset in far_first:
        send_rows(half - 1, span, offset)
    gather_batch(half - 2)

    hd = nz * hb
    rows_p = nz * own
    groups = 128 // rank
    high = rows_p // groups
    for block in late_blocks:
        total_m[at(block)] = jnp.zeros((own, width), F32)

    def pack(x):
        return jnp.concatenate([x[k * high : (k + 1) * high] for k in range(groups)], axis=1)

    def unpack(x):
        return jnp.concatenate([x[:, k * rank : (k + 1) * rank] for k in range(groups)], axis=0)

    deep_p[z] = pack(dot3(total_m[...].reshape(rows_p, width), q_parts, NT))
    exchange_z(1, deep_p.at[z], deep_p)
    landed(0, nd, late_land)
    late_p[z] = jnp.sum(late_land[...], axis=0)
    exchange_z(5 + half, late_p.at[z], late_p)
    gather_batch(half - 1)
    m = split2(total_m[...].reshape(rows_p, width))
    landed(1, nz, deep_p)
    early = unpack(jnp.sum(deep_p[...], axis=0))
    landed(5 + half, nz, late_p)
    mine = early
    for k, block in enumerate(late_blocks):
        x = late_p[...][:, :, k * rank : (k + 1) * rank]
        shift = -block % nz
        x = jnp.concatenate([x[shift:], x[:shift]], axis=0)
        mine = mine + x.reshape(rows_p, rank)
    packed = pack(mine)
    full_p[dp] = packed

    ut = dot3(mine, m, TN)
    urows = part_u.shape[1]
    utiles = width // 128
    for i in range(rank // urows):
        for j in range(utiles):
            part_u[i * utiles + j] = ut[i * urows : (i + 1) * urows, j * 128 : j * 128 + 128]
    plane_u[dp] = part_u[dp]
    exchange_dp(3, lambda there: part_u.at[there], plane_u)
    exchange_dp(2, lambda there: full_p.at[dp], full_p)
    landed(3, nd, plane_u)
    full_u[dp] = jnp.sum(plane_u[...], axis=0)
    exchange_dp(4, lambda there: full_u.at[dp], full_u)
    landed(2, nd, full_p)
    for j in range(nd):
        natural_p[:, j * own : (j + 1) * own] = unpack(full_p[j]).reshape(nz, own, rank)
    p = natural_p[...].reshape(hd, rank)

    gram = lax.dot_general(p, p, TN, precision=HIGHEST, preferred_element_type=F32)
    row_id = lax.broadcasted_iota(jnp.int32, (rank, 1), 0)
    eye = (
        lax.broadcasted_iota(jnp.int32, (rank, rank), 0)
        == lax.broadcasted_iota(jnp.int32, (rank, rank), 1)
    ).astype(F32)
    x = jnp.concatenate([gram, eye], axis=1)

    def eliminate(x, start, stop):
        for k in range(start, stop):
            d = x[k : k + 1, k : k + 1]
            r = lax.rsqrt(d)
            r = r * (1.5 - 0.5 * d * r * r)
            row = x[k : k + 1, :] * r
            column = x[:, k : k + 1] * r
            x = jnp.where(row_id == k, row, jnp.where(row_id > k, x - column * row, x))
        return x

    x = eliminate(x, 0, rank)
    inverse = x[:, rank:]
    square = lax.dot_general(inverse, inverse, TN, precision=HIGHEST, preferred_element_type=F32)
    joint = jnp.concatenate([inverse, square / nd], axis=0)
    p1, p2 = split2(p)
    left_side[...] = jnp.concatenate([p1, p1, p2], axis=1)
    def sent(s, carry):
        for piece in range(PIECES):
            for way in range(2):
                ring(way, s, piece).wait_send()
        return carry

    lax.fori_loop(0, half - 1, sent, 0)
    for piece in range(PIECES):
        ring(0 if piece < PIECES // 2 else 1, half - 1, piece).wait_send()
    for batch in range(half):
        rest = plane_m.at[pl.ds(0, nd - 1), pl.ds(starts[batch], counts[batch])]
        pltpu.make_async_copy(rest, rest, send_sem.at[5 + batch]).wait()
    left(0, nd, late_land)
    left(1, nz, deep_p)
    left(5 + half, nz, late_p)
    left(2, nd, full_p)
    left(3, nd, plane_u)
    landed(4, nd, full_u)
    ut = jnp.concatenate(
        [
            jnp.concatenate([full_u[i * utiles + j] for j in range(utiles)], axis=1)
            for i in range(rank // urows)
        ],
        axis=0,
    )
    both = lax.dot_general(joint, ut, NN, precision=HIGHEST, preferred_element_type=F32)
    fqt = both[:rank]
    fq[...] = fqt
    m1, m2 = split2(both[rank:])
    right_side[...] = jnp.concatenate([m1, m2, m1], axis=0)
    left(4, nd, full_u)


def finish(fq, merged, left_side, right_side, fq_hbm, new_hbm, out, store_sem):
    nz, hb, width = out.shape
    stores = [pltpu.make_async_copy(fq, fq_hbm, store_sem.at[0])]
    stores[0].start()
    per = nz // GROUPS
    for g in range(GROUPS):
        low = jnp.dot(
            left_side[g * per * hb : (g + 1) * per * hb],
            right_side[...],
            preferred_element_type=F32,
        )
        span = pl.ds(g * per, per)
        out[span] = (merged[span] - low.reshape(per, hb, width)).astype(BF16)
        stores.append(pltpu.make_async_copy(out.at[span], new_hbm.at[span], store_sem.at[1 + g]))
        stores[-1].start()
    for store in stores:
        store.wait()


def local(nd, nz, tokens, grad_out, error_old, power_q):
    tok_n, hb = grad_out.shape
    width = tokens.shape[1]
    rank = power_q.shape[1]
    hd = hb * nz
    chunk = rank * hd // nd // 128
    urows = rank * width // nd // 128
    operands = (grad_out.T, tokens, error_old.reshape(nz, hb, width), power_q.T)
    any_space = pl.BlockSpec(memory_space=pl.ANY)
    held = pl.pallas_call(
        functools.partial(kernel, nd, nz),
        out_shape=(
            pltpu.VMEM((rank, width), F32),
            pltpu.VMEM((nz, hb, width), F32),
            pltpu.VMEM((hd, 3 * rank), BF16),
            pltpu.VMEM((3 * rank, width), BF16),
        ),
        in_specs=[any_space] * 4,
        out_specs=(pl.BlockSpec(memory_space=pltpu.VMEM),) * 4,
        scratch_shapes=[
            pltpu.VMEM((nz, hb, tok_n), BF16),
            pltpu.VMEM((tok_n, width), BF16),
            pltpu.VMEM((nz, hb, width), BF16),
            pltpu.VMEM((rank, width), F32),
            pltpu.VMEM((nd, nz, hb // nd, width), F32),
            pltpu.VMEM((nd, nz, hb // nd, width), F32),
            pltpu.VMEM((nz, hb // nd, width), F32),
            pltpu.VMEM((nd, hb // nd, 128), F32),
            pltpu.VMEM((nd, hb // nd, 128), F32),
            pltpu.VMEM((nz, chunk, 128), F32),
            pltpu.VMEM((nz, hb // nd, 128), F32),
            pltpu.VMEM((nd, chunk, 128), F32),
            pltpu.VMEM((nz, hb, rank), F32),
            pltpu.VMEM((nd, urows, 128), F32),
            pltpu.VMEM((nd, urows, 128), F32),
            pltpu.VMEM((nd, urows, 128), F32),
            pltpu.SemaphoreType.DMA((4,)),
            pltpu.SemaphoreType.DMA((2, nz // 2, PIECES)),
            pltpu.SemaphoreType.DMA((2, nz // 2, PIECES)),
            pltpu.SemaphoreType.DMA((6 + nz // 2,)),
            pltpu.SemaphoreType.DMA((6 + nz // 2,)),
        ],
        compiler_params=pltpu.CompilerParams(
            collective_id=0, has_side_effects=True, vmem_limit_bytes=44 * 1024 * 1024
        ),
    )(*(pltpu.with_memory_space_constraint(a, pltpu.HBM) for a in operands))
    fqt, new = pl.pallas_call(
        finish,
        out_shape=(pltpu.HBM((rank, width), F32), pltpu.HBM((nz, hb, width), BF16)),
        in_specs=[pl.BlockSpec(memory_space=pltpu.VMEM)] * 4,
        out_specs=(any_space, any_space),
        scratch_shapes=[
            pltpu.VMEM((nz, hb, width), BF16),
            pltpu.SemaphoreType.DMA((1 + GROUPS,)),
        ],
        compiler_params=pltpu.CompilerParams(vmem_limit_bytes=8 * 1024 * 1024),
    )(*(pltpu.with_memory_space_constraint(a, pltpu.VMEM) for a in held))
    return fqt.T, new.reshape(1, hd, width)


def solution(mesh):
    placed = (P("dp", "tensor"), P("dp", "tensor"), P("dp", None, "tensor"), P("tensor", None))
    return jax.shard_map(
        functools.partial(local, mesh.shape["dp"], mesh.shape["tensor"]),
        mesh=mesh,
        in_specs=placed,
        out_specs=(P("tensor", None), P("dp", None, "tensor")),
        check_vma=False,
    )
```

```python
import functools
import math

import jax
import jax.numpy as jnp
from jax import lax
from jax.experimental import pallas as pl
from jax.experimental.pallas import tpu as pltpu
from jax.sharding import PartitionSpec as P

F32 = jnp.float32
BF16 = jnp.bfloat16
MESH = pl.DeviceIdType.MESH
HIGHEST = lax.Precision.HIGHEST
GROUPS = 4
NT = (((1,), (1,)), ((), ()))
NN = (((1,), (0,)), ((), ()))
TN = (((0,), (0,)), ((), ()))
PIECES = 4


def split2(x):
    hi = x.astype(BF16)
    return hi, (x - hi.astype(F32)).astype(BF16)


def dot3(a, b, dims):
    a1, a2 = split2(a)
    b1, b2 = b if isinstance(b, tuple) else split2(b)
    dot = functools.partial(lax.dot_general, dimension_numbers=dims, preferred_element_type=F32)
    return dot(a1, b1) + (dot(a1, b2) + dot(a2, b1))


def kernel(
    nd, nz, gt_hbm, tok_hbm, err_hbm, qt_hbm, fq, merged, left_side, right_side,
    gt, tok, err, qt,
    stage, plane_m, total_m, late_part, late_land, deep_p, late_p, full_p, natural_p,
    part_u, plane_u, full_u,
    load_sem, ring_send, ring_recv, send_sem, recv_sem,
):
    dp = lax.axis_index("dp")
    z = lax.axis_index("tensor")
    hb = gt.shape[1]
    rows = hb // PIECES
    half = nz // 2
    rank, width = qt.shape
    q = qt
    own = hb // nd
    across = math.isqrt(nd // 2)
    place = (dp // (2 * across), lax.rem(dp // 2, across), lax.rem(dp, 2))
    offsets = [(i, j, k) for i in range(across) for j in range(across) for k in range(2)][1:]
    far_first = sorted(offsets, key=lambda o: -sum(min(v, across - v) for v in o[:2]))

    def peer(offset):
        x, y, core = ((p + o) & (n - 1) for p, o, n in zip(place, offset, (across, across, 2)))
        return (x * across + y) * 2 + core

    loads = [
        pltpu.make_async_copy(gt_hbm, gt.at[z], load_sem.at[0]),
        pltpu.make_async_copy(tok_hbm, tok, load_sem.at[1]),
        pltpu.make_async_copy(err_hbm, err, load_sem.at[2]),
        pltpu.make_async_copy(qt_hbm, qt, load_sem.at[3]),
    ]
    loads[0].start()

    barrier = pltpu.get_barrier_semaphore()
    for step in (1, nz - 1):
        pl.semaphore_signal(
            barrier, inc=1, device_id={"tensor": lax.rem(z + step, nz)}, device_id_type=MESH
        )
    for offset in far_first:
        pl.semaphore_signal(barrier, inc=1, device_id={"dp": peer(offset)}, device_id_type=MESH)
    for load in loads[1:]:
        load.start()
    pl.semaphore_wait(barrier, nd + 1)

    def ring(way, step, piece):
        sign = 1 if way == 0 else -1
        block = lax.rem(z - sign * step + 2 * nz, nz)
        there = lax.rem(z + sign + nz, nz)
        ref = gt.at[block, pl.ds(piece * rows, rows)]
        return pltpu.make_async_remote_copy(
            src_ref=ref,
            dst_ref=ref,
            send_sem=ring_send.at[way, step, piece],
            recv_sem=ring_recv.at[way, step, piece],
            device_id={"tensor": there},
            device_id_type=MESH,
        )

    def arrived(way, step, piece):
        sign = 1 if way == 0 else -1
        block = lax.rem(z - sign * (step + 1) + 2 * nz, nz)
        ref = gt.at[block, pl.ds(piece * rows, rows)]
        pltpu.make_async_copy(ref, ref, ring_recv.at[way, step, piece]).wait()

    def exchange_dp(sems, source, target):
        for offset in far_first:
            there = peer(offset)
            pltpu.make_async_remote_copy(
                src_ref=source(there),
                dst_ref=target.at[dp],
                send_sem=send_sem.at[sems],
                recv_sem=recv_sem.at[sems],
                device_id={"dp": there},
                device_id_type=MESH,
            ).start()

    def exchange_z(sems, source, target):
        for offset in sorted(range(1, nz), key=lambda k: -min(k, nz - k)):
            pltpu.make_async_remote_copy(
                src_ref=source,
                dst_ref=target.at[z],
                send_sem=send_sem.at[sems],
                recv_sem=recv_sem.at[sems],
                device_id={"tensor": lax.rem(z + offset, nz)},
                device_id_type=MESH,
            ).start()

    def landed(sems, n, target):
        rest = target.at[pl.ds(0, n - 1)]
        pltpu.make_async_copy(rest, rest, recv_sem.at[sems]).wait()

    def left(sems, n, target):
        rest = target.at[pl.ds(0, n - 1)]
        pltpu.make_async_copy(rest, rest, send_sem.at[sems]).wait()

    def at(offset):
        return lax.rem(z + offset + 2 * nz, nz)

    def multiply(*blocks):
        x = [gt[block] for block in blocks]
        x = x[0] if len(x) == 1 else jnp.concatenate(x, axis=0)
        y = jnp.dot(x, tok[...], preferred_element_type=F32)
        parts = []
        for i, block in enumerate(blocks):
            part = y[i * hb : (i + 1) * hb] + err[block].astype(F32)
            merged[block] = part
            parts.append(part.reshape(nd, own, width))
        return parts

    slots = {}
    for step in range(half):
        for block in (0,) if step == 0 else (step, -step) + (half,) * (step == half - 1):
            batch = step
            slots[block] = (batch, sum(1 for b in slots.values() if b[0] == batch))
    counts = [sum(1 for b in slots.values() if b[0] == k) for k in range(half)]
    starts = [sum(counts[:k]) for k in range(half)]

    pending = []

    def send_rows(batch, span, offset):
        there = peer(offset)
        pltpu.make_async_remote_copy(
            src_ref=stage.at[there, span],
            dst_ref=plane_m.at[dp, span],
            send_sem=send_sem.at[5 + batch],
            recv_sem=recv_sem.at[5 + batch],
            device_id={"dp": there},
            device_id_type=MESH,
        ).start()

    def send_pending(n):
        for _ in range(min(n, len(pending))):
            pending.pop(0)()

    def put(step):
        blocks = (0,) if step == 0 else (step, -step)
        for block, part in zip(blocks, multiply(*(at(b) for b in blocks)), strict=True):
            batch, slot = slots[block]
            stage[:, starts[batch] + slot] = part
        if step < half - 1:
            span = pl.ds(starts[step], counts[step])
            plane_m[dp, span] = stage[dp, span]
            for offset in far_first:
                pending.append(functools.partial(send_rows, step, span, offset))

    def gather_batch(batch):
        span = pl.ds(starts[batch], counts[batch])
        rest = plane_m.at[pl.ds(0, nd - 1), span]
        pltpu.make_async_copy(rest, rest, recv_sem.at[5 + batch]).wait()
        for block, (b, slot) in slots.items():
            if b == batch:
                total_m[at(block)] = jnp.sum(plane_m[:, starts[b] + slot], axis=0)

    loads[0].wait()
    for piece in range(PIECES):
        ring(0, 0, piece).start()
        ring(1, 0, piece).start()
    for load in loads[1:]:
        load.wait()
    put(0)
    for s in range(1, half):
        for piece in range(PIECES):
            for way in range(2):
                arrived(way, s - 1, piece)
                if s < half - 1 or (piece < PIECES // 2) == (way == 0):
                    ring(way, s, piece).start()
            send_pending(nd // PIECES if piece < PIECES - 1 else nd)
        put(s)
        if s > 1:
            gather_batch(s - 2)
    late_blocks = (half - 1, 1 - half, half)
    q_parts = split2(q[...])
    late = [dot3(merged[at(block)], q_parts, NT) for block in late_blocks[:2]]
    for piece in range(PIECES):
        arrived(0 if piece < PIECES // 2 else 1, half - 1, piece)
    part = multiply(at(half))[0]
    late.append(dot3(merged[at(half)], q_parts, NT))
    late = [x.reshape(nd, own, rank) for x in late] + [jnp.zeros((nd, own, 128 - 3 * rank), F32)]
    late_part[...] = jnp.concatenate(late, axis=2)
    late_land[dp] = late_part[dp]
    exchange_dp(0, lambda there: late_part.at[there], late_land)
    stage[:, starts[half - 1] + 2] = part
    span = pl.ds(starts[half - 1], counts[half - 1])
    plane_m[dp, span] = stage[dp, span]
    for offset in far_first:
        send_rows(half - 1, span, offset)
    gather_batch(half - 2)

    hd = nz * hb
    rows_p = nz * own
    groups = 128 // rank
    high = rows_p // groups
    for block in late_blocks:
        total_m[at(block)] = jnp.zeros((own, width), F32)

    def pack(x):
        return jnp.concatenate([x[k * high : (k + 1) * high] for k in range(groups)], axis=1)

    def unpack(x):
        return jnp.concatenate([x[:, k * rank : (k + 1) * rank] for k in range(groups)], axis=0)

    deep_p[z] = pack(dot3(total_m[...].reshape(rows_p, width), q_parts, NT))
    exchange_z(1, deep_p.at[z], deep_p)
    landed(0, nd, late_land)
    late_p[z] = jnp.sum(late_land[...], axis=0)
    exchange_z(5 + half, late_p.at[z], late_p)
    gather_batch(half - 1)
    m = split2(total_m[...].reshape(rows_p, width))
    landed(1, nz, deep_p)
    early = unpack(jnp.sum(deep_p[...], axis=0))
    landed(5 + half, nz, late_p)
    mine = early
    for k, block in enumerate(late_blocks):
        x = late_p[...][:, :, k * rank : (k + 1) * rank]
        shift = -block % nz
        x = jnp.concatenate([x[shift:], x[:shift]], axis=0)
        mine = mine + x.reshape(rows_p, rank)

    ut = dot3(mine, m, TN)
    urows = part_u.shape[1]
    utiles = width // 128
    for i in range(rank // urows):
        for j in range(utiles):
            part_u[i * utiles + j] = ut[i * urows : (i + 1) * urows, j * 128 : j * 128 + 128]
    plane_u[dp] = part_u[dp]
    exchange_dp(3, lambda there: part_u.at[there], plane_u)
    full_p[dp] = pack(mine)
    exchange_dp(2, lambda there: full_p.at[dp], full_p)
    landed(3, nd, plane_u)
    full_u[dp] = jnp.sum(plane_u[...], axis=0)
    exchange_dp(4, lambda there: full_u.at[dp], full_u)
    landed(2, nd, full_p)
    for j in range(nd):
        natural_p[:, j * own : (j + 1) * own] = unpack(full_p[j]).reshape(nz, own, rank)
    p = natural_p[...].reshape(hd, rank)

    gram = lax.dot_general(p, p, TN, precision=HIGHEST, preferred_element_type=F32)
    row_id = lax.broadcasted_iota(jnp.int32, (rank, 1), 0)
    eye = (
        lax.broadcasted_iota(jnp.int32, (rank, rank), 0)
        == lax.broadcasted_iota(jnp.int32, (rank, rank), 1)
    ).astype(F32)
    x = jnp.concatenate([gram, eye], axis=1)

    def eliminate(x, start, stop):
        for k in range(start, stop):
            d = x[k : k + 1, k : k + 1]
            r = lax.rsqrt(d)
            r = r * (1.5 - 0.5 * d * r * r)
            row = x[k : k + 1, :] * r
            column = x[:, k : k + 1] * r
            x = jnp.where(row_id == k, row, jnp.where(row_id > k, x - column * row, x))
        return x

    x = eliminate(x, 0, rank)
    inverse = x[:, rank:]
    square = lax.dot_general(inverse, inverse, TN, precision=HIGHEST, preferred_element_type=F32)
    joint = jnp.concatenate([inverse, square / nd], axis=0)
    p1, p2 = split2(p)
    left_side[...] = jnp.concatenate([p1, p1, p2], axis=1)
    def sent(s, carry):
        for piece in range(PIECES):
            for way in range(2):
                ring(way, s, piece).wait_send()
        return carry

    lax.fori_loop(0, half - 1, sent, 0)
    for piece in range(PIECES):
        ring(0 if piece < PIECES // 2 else 1, half - 1, piece).wait_send()
    for batch in range(half):
        rest = plane_m.at[pl.ds(0, nd - 1), pl.ds(starts[batch], counts[batch])]
        pltpu.make_async_copy(rest, rest, send_sem.at[5 + batch]).wait()
    left(0, nd, late_land)
    left(1, nz, deep_p)
    left(5 + half, nz, late_p)
    left(2, nd, full_p)
    left(3, nd, plane_u)
    landed(4, nd, full_u)
    ut = jnp.concatenate(
        [
            jnp.concatenate([full_u[i * utiles + j] for j in range(utiles)], axis=1)
            for i in range(rank // urows)
        ],
        axis=0,
    )
    both = lax.dot_general(joint, ut, NN, precision=HIGHEST, preferred_element_type=F32)
    fqt = both[:rank]
    fq[...] = fqt
    m1, m2 = split2(both[rank:])
    right_side[...] = jnp.concatenate([m1, m2, m1], axis=0)
    left(4, nd, full_u)


def finish(fq, merged, left_side, right_side, fq_hbm, new_hbm, out, store_sem):
    nz, hb, width = out.shape
    stores = [pltpu.make_async_copy(fq, fq_hbm, store_sem.at[0])]
    stores[0].start()
    per = nz // GROUPS
    for g in range(GROUPS):
        low = jnp.dot(
            left_side[g * per * hb : (g + 1) * per * hb],
            right_side[...],
            preferred_element_type=F32,
        )
        span = pl.ds(g * per, per)
        out[span] = (merged[span] - low.reshape(per, hb, width)).astype(BF16)
        stores.append(pltpu.make_async_copy(out.at[span], new_hbm.at[span], store_sem.at[1 + g]))
        stores[-1].start()
    for store in stores:
        store.wait()


def local(nd, nz, tokens, grad_out, error_old, power_q):
    tok_n, hb = grad_out.shape
    width = tokens.shape[1]
    rank = power_q.shape[1]
    hd = hb * nz
    chunk = rank * hd // nd // 128
    urows = rank * width // nd // 128
    operands = (grad_out.T, tokens, error_old.reshape(nz, hb, width), power_q.T)
    any_space = pl.BlockSpec(memory_space=pl.ANY)
    held = pl.pallas_call(
        functools.partial(kernel, nd, nz),
        out_shape=(
            pltpu.VMEM((rank, width), F32),
            pltpu.VMEM((nz, hb, width), F32),
            pltpu.VMEM((hd, 3 * rank), BF16),
            pltpu.VMEM((3 * rank, width), BF16),
        ),
        in_specs=[any_space] * 4,
        out_specs=(pl.BlockSpec(memory_space=pltpu.VMEM),) * 4,
        scratch_shapes=[
            pltpu.VMEM((nz, hb, tok_n), BF16),
            pltpu.VMEM((tok_n, width), BF16),
            pltpu.VMEM((nz, hb, width), BF16),
            pltpu.VMEM((rank, width), F32),
            pltpu.VMEM((nd, nz, hb // nd, width), F32),
            pltpu.VMEM((nd, nz, hb // nd, width), F32),
            pltpu.VMEM((nz, hb // nd, width), F32),
            pltpu.VMEM((nd, hb // nd, 128), F32),
            pltpu.VMEM((nd, hb // nd, 128), F32),
            pltpu.VMEM((nz, chunk, 128), F32),
            pltpu.VMEM((nz, hb // nd, 128), F32),
            pltpu.VMEM((nd, chunk, 128), F32),
            pltpu.VMEM((nz, hb, rank), F32),
            pltpu.VMEM((nd, urows, 128), F32),
            pltpu.VMEM((nd, urows, 128), F32),
            pltpu.VMEM((nd, urows, 128), F32),
            pltpu.SemaphoreType.DMA((4,)),
            pltpu.SemaphoreType.DMA((2, nz // 2, PIECES)),
            pltpu.SemaphoreType.DMA((2, nz // 2, PIECES)),
            pltpu.SemaphoreType.DMA((6 + nz // 2,)),
            pltpu.SemaphoreType.DMA((6 + nz // 2,)),
        ],
        compiler_params=pltpu.CompilerParams(
            collective_id=0, has_side_effects=True, vmem_limit_bytes=44 * 1024 * 1024
        ),
    )(*(pltpu.with_memory_space_constraint(a, pltpu.HBM) for a in operands))
    fqt, new = pl.pallas_call(
        finish,
        out_shape=(pltpu.HBM((rank, width), F32), pltpu.HBM((nz, hb, width), BF16)),
        in_specs=[pl.BlockSpec(memory_space=pltpu.VMEM)] * 4,
        out_specs=(any_space, any_space),
        scratch_shapes=[
            pltpu.VMEM((nz, hb, width), BF16),
            pltpu.SemaphoreType.DMA((1 + GROUPS,)),
        ],
        compiler_params=pltpu.CompilerParams(vmem_limit_bytes=8 * 1024 * 1024),
    )(*(pltpu.with_memory_space_constraint(a, pltpu.VMEM) for a in held))
    return fqt.T, new.reshape(1, hd, width)


def solution(mesh):
    placed = (P("dp", "tensor"), P("dp", "tensor"), P("dp", None, "tensor"), P("tensor", None))
    return jax.shard_map(
        functools.partial(local, mesh.shape["dp"], mesh.shape["tensor"]),
        mesh=mesh,
        in_specs=placed,
        out_specs=(P("tensor", None), P("dp", None, "tensor")),
        check_vma=False,
    )
```
